512 devices in a mesh: member: 8 (over y_lo, core), space: 64 (over z, x, y_hi).
Axes of the slice: x: 4, y: 8 (y_hi: 2, y_lo: 4; y = y_hi * 4 + y_lo), z: 8, core: 2. Of those that a mesh axis runs over, the one named last changes fastest.
Arguments:
- latent: bfloat16 [8, 8192, 1024], P('member', 'space'), may hold values from -6 to 6
- w_query: bfloat16 [1024, 512], replicated, may hold values from -0.1875 to 0.1875
- w_key: bfloat16 [1024, 512], replicated, may hold values from -0.1875 to 0.1875
- w_value: bfloat16 [1024, 512], replicated, may hold values from -0.1875 to 0.1875
- w_out: bfloat16 [512, 1024], replicated, may hold values from -0.25 to 0.25
- w_decode: bfloat16 [100, 1024], replicated, may hold values from -0.1875 to 0.1875
- window: int32 [8192, 32], P('space'), may hold values from 0 to 8191, as said below
- decoder_src: int32 [32768, 3], P('space'), may hold values from 0 to 8191, as said below
- edge_weight: float32 [32768, 3], P('space'), may hold values from 0.3 to 1
- target: bfloat16 [100, 32768], P(None, 'space'), may hold values from -6 to 6
- area: float32 [32768], P('space'), may hold values from 0.5 to 2
Outputs:
- latent_grad: bfloat16 [8, 8192, 1024], P('member', 'space')
The draws below stay inside these ranges and needn't reach their ends.
Inputs may be any that keep to these rules, and one draw needn't show every extreme that they name: `window`: every entry of row i lies within 64 of i; every row lists i - 64 and i + 64 where these rows exist, the other entries are clipped to the grid. `decoder_src`: for grid point g the entries lie within 64 of the centre (g // 512) * 128 + ((g % 512) * 128) // 512; each point lists centre - 64 and centre + 64 where these rows exist, clipped to the grid.
All inputs are finite; a program needn't handle non-finite values.
Results may differ from the reference program's by a relative error of at most 0.04.
Values may be sent and summed in bfloat16 or wider, within the bound.
A program may use at most 64 MiB of HBM per device.

```python
import math
import jax
import jax.numpy as jnp
from jax import lax

D = 1024
HEADS = 8
DH = 64
V = 100
R = 64
KW = 32
KD = 3
L_DEV = 128
G_DEV = 512
MEMBERS = 8
LAT = 8192
GRID = 32768


def draw_window(key, part):
    key = jax.random.fold_in(key, 11)
    latent_rows = jnp.arange(LAT, dtype=jnp.int32)[:, None]
    shifts = jax.random.randint(key, (LAT, KW), -R, R + 1, dtype=jnp.int32)
    column = jnp.arange(KW, dtype=jnp.int32)[None, :]
    shifts = jnp.where(column == 0, -R, jnp.where(column == 1, R, shifts))
    return jnp.clip(latent_rows + shifts, 0, LAT - 1).astype(jnp.int32)


def draw_decoder_src(key, part):
    key = jax.random.fold_in(key, 23)
    points = jnp.arange(GRID, dtype=jnp.int32)
    centre = points // G_DEV * L_DEV + points % G_DEV * L_DEV // G_DEV
    shifts = jax.random.randint(key, (GRID, KD), -R, R + 1, dtype=jnp.int32)
    column = jnp.arange(KD, dtype=jnp.int32)[None, :]
    shifts = jnp.where(column == 0, -R, jnp.where(column == 1, R, shifts))
    return jnp.clip(centre[:, None] + shifts, 0, LAT - 1).astype(jnp.int32)


def block_levels(stream_key, extent, shards, least, largest):
    factor_of = 1.0
    for dim, parts in shards:
        draws = jax.random.uniform(jax.random.fold_in(jax.random.fold_in(stream_key, 6), dim), (parts,), jnp.float32, least / len(shards), largest / len(shards))
        factor_of = factor_of * jnp.repeat(jnp.exp(draws), extent[dim] // parts).reshape((-1,) + (1,) * (len(extent) - 1 - dim))
    return factor_of


def bell_draw(key, shape, spread, most, pieces=(), kind=jnp.bfloat16):
    values = spread * jax.random.normal(key, shape, jnp.float32)
    if pieces:
        values = values * block_levels(key, shape, pieces, -0.22, 0.18)
    return jnp.clip(values, -most, most).astype(kind)


def setup_inputs(seed: int = 0) -> dict:
    seeds = jax.random.split(jax.random.key(seed), 12)
    latent = bell_draw(seeds[0], (MEMBERS, LAT, D), 1.0, 6.0, ((0, 8), (1, 64)))
    w_query = bell_draw(seeds[1], (D, HEADS * DH), D ** -0.5, 0.1875)
    w_key = bell_draw(seeds[2], (D, HEADS * DH), D ** -0.5, 0.1875)
    w_value = bell_draw(seeds[3], (D, HEADS * DH), D ** -0.5, 0.1875)
    w_out = bell_draw(seeds[4], (HEADS * DH, D), (HEADS * DH) ** -0.5, 0.25)
    w_decode = bell_draw(seeds[5], (V, D), D ** -0.5, 0.1875)
    window = draw_window(jax.random.fold_in(seeds[11], 71), 0)
    decoder_src = draw_decoder_src(jax.random.fold_in(seeds[11], 71), 0)
    edge_weight = jnp.clip(jnp.exp(math.log(1.0) - 1.2039728 * jax.random.uniform(seeds[8], (GRID, KD), jnp.float32) ** block_levels(seeds[8], (GRID, KD), ((0, 64),), -0.2, 0.2)), 0.3, 1.0)
    target = bell_draw(seeds[9], (V, GRID), 1.0, 6.0, ((1, 64),))
    area = jnp.clip(jnp.exp(math.log(2.0) - 1.3862944 * jax.random.uniform(seeds[10], (GRID,), jnp.float32) ** block_levels(seeds[10], (GRID,), ((0, 64),), -0.2, 0.2)), 0.5, 2.0)
    return dict(latent=latent, w_query=w_query, w_key=w_key, w_value=w_value, w_out=w_out, w_decode=w_decode, window=window, decoder_src=decoder_src, edge_weight=edge_weight, target=target, area=area)


score_scale = 6.0
eps_norm = 1e-06
delta_smooth = 0.1

def widen(array):
    return array.astype(jnp.float32)

def normalize_heads(projected):
    grouped = projected.reshape(projected.shape[0], HEADS, DH)
    factor = lax.rsqrt(lax.optimization_barrier(jnp.mean(grouped * grouped, axis=2, keepdims=True)) + eps_norm)
    return (grouped * factor, factor)

def norm_backward(grad_hat, unit_rows, factor):
    return factor * (grad_hat - unit_rows * lax.optimization_barrier(jnp.mean(grad_hat * unit_rows, axis=2, keepdims=True)))

def smooth_slope(difference):
    return difference * lax.rsqrt(difference * difference + delta_smooth * delta_smooth)

def block_probs(query_low, key_low, local_index):
    count_query = query_low.shape[0]
    count_key = key_low.shape[0]
    counts = jnp.zeros((count_query, count_key), jnp.float32).at[jnp.arange(count_query).astype(jnp.int32)[:, None], local_index].add(1.0)
    scores = jnp.einsum('qhd,khd->hqk', widen(query_low), widen(key_low)) * (score_scale / DH)
    weighted = counts[None] * jnp.exp(scores)
    probs = weighted / lax.optimization_barrier(jnp.sum(weighted, axis=2, keepdims=True))
    return (probs, probs.astype(jnp.bfloat16))

def member_layer(hidden, w_query, w_key, w_value, w_out, window):
    queries = jnp.dot(hidden, w_query, preferred_element_type=jnp.float32)
    key_proj = jnp.dot(hidden, w_key, preferred_element_type=jnp.float32)
    value_low = jnp.dot(hidden, w_value, preferred_element_type=jnp.float32).astype(jnp.bfloat16).reshape(LAT, HEADS, DH)
    query_hat, query_factor = normalize_heads(queries)
    key_hat, key_factor = normalize_heads(key_proj)
    query_low = query_hat.astype(jnp.bfloat16)
    key_low = key_hat.astype(jnp.bfloat16)
    key_pad = jnp.pad(key_low, ((R, R), (0, 0), (0, 0)))
    value_pad = jnp.pad(value_low, ((R, R), (0, 0), (0, 0)))

    def block_inputs(block):
        first = (block * L_DEV).astype(jnp.int32)
        query_block = lax.dynamic_slice_in_dim(query_low, first, L_DEV, 0)
        key_block = lax.dynamic_slice_in_dim(key_pad, first, L_DEV + 2 * R, 0)
        value_block = lax.dynamic_slice_in_dim(value_pad, first, L_DEV + 2 * R, 0)
        local_index = lax.dynamic_slice_in_dim(window, first, L_DEV, 0) - (first - R)
        return (first, query_block, key_block, value_block, local_index)

    def forward_block(block):
        first, query_block, key_block, value_block, local_index = block_inputs(block)
        probs, probs_low = block_probs(query_block, key_block, local_index)
        mixed = jnp.einsum('hqk,khd->qhd', widen(probs_low), widen(value_block)).astype(jnp.bfloat16)
        return mixed.reshape(L_DEV, HEADS * DH)
    blocks = jnp.arange(LAT // L_DEV).astype(jnp.int32)
    mixed = lax.map(forward_block, blocks).reshape(LAT, HEADS * DH)
    output = (widen(hidden) + jnp.dot(mixed, w_out, preferred_element_type=jnp.float32)).astype(jnp.bfloat16)
    saved = (query_hat, query_factor, key_hat, key_factor, block_inputs, blocks)
    return (output, saved)

def member_backward(hidden, dout, saved, w_query, w_key, w_value, w_out):
    query_hat, query_factor, key_hat, key_factor, block_inputs, blocks = saved
    dout_low = dout.astype(jnp.bfloat16)
    dmixed = jnp.dot(dout_low, w_out.T, preferred_element_type=jnp.float32).astype(jnp.bfloat16).reshape(LAT, HEADS, DH)

    def backward_block(block):
        first, query_block, key_block, value_block, local_index = block_inputs(block)
        probs, probs_low = block_probs(query_block, key_block, local_index)
        dmixed_block = lax.dynamic_slice_in_dim(dmixed, first, L_DEV, 0)
        dprob = jnp.einsum('qhd,khd->hqk', widen(dmixed_block), widen(value_block))
        row_term = lax.optimization_barrier(jnp.sum(probs * dprob, axis=2, keepdims=True))
        dscore = (probs * (dprob - row_term)).astype(jnp.bfloat16)
        dq_hat = jnp.einsum('hqk,khd->qhd', widen(dscore), widen(key_block)) * (score_scale / DH)
        dk_hat = jnp.einsum('hqk,qhd->khd', widen(dscore), widen(query_block)) * (score_scale / DH)
        dvalue = jnp.einsum('hqk,qhd->khd', widen(probs_low), widen(dmixed_block))
        return (dq_hat, jnp.concatenate([dk_hat, dvalue], axis=2))
    dq_blocks, key_parts = lax.map(backward_block, blocks)
    dq_hat = dq_blocks.reshape(LAT, HEADS, DH)
    middle = key_parts[:, R:R + L_DEV]
    left_part = key_parts[:, :R]
    right_part = key_parts[:, L_DEV + R:]
    zero_part = jnp.zeros_like(left_part[:1])
    from_next = jnp.concatenate([left_part[1:], zero_part], axis=0)
    from_prev = jnp.concatenate([zero_part, right_part[:-1]], axis=0)
    total = middle.at[:, L_DEV - R:].add(from_next).at[:, :R].add(from_prev)
    total = total.reshape(LAT, HEADS, 2 * DH)
    dq_low = norm_backward(dq_hat, query_hat, query_factor).reshape(LAT, HEADS * DH).astype(jnp.bfloat16)
    dk_low = norm_backward(total[:, :, :DH], key_hat, key_factor).reshape(LAT, HEADS * DH).astype(jnp.bfloat16)
    dvalue_low = total[:, :, DH:].reshape(LAT, HEADS * DH).astype(jnp.bfloat16)
    grad = dout + jnp.dot(dq_low, w_query.T, preferred_element_type=jnp.float32)
    grad = grad + jnp.dot(dk_low, w_key.T, preferred_element_type=jnp.float32)
    grad = grad + jnp.dot(dvalue_low, w_value.T, preferred_element_type=jnp.float32)
    return grad.astype(jnp.bfloat16)

def reference(latent, w_query, w_key, w_value, w_out, w_decode, window, decoder_src, edge_weight, target, area):
    outputs_saved = []
    predictions = []
    for member in range(MEMBERS):
        output, saved = member_layer(latent[member], w_query, w_key, w_value, w_out, window)
        outputs_saved.append(saved)
        gathered_sum = jnp.zeros((GRID, D), jnp.float32)
        for slot in range(KD):
            gathered_sum = gathered_sum + edge_weight[:, slot, None] * widen(output[decoder_src[:, slot]])
        aggregate = gathered_sum.astype(jnp.bfloat16)
        predictions.append(jnp.dot(w_decode, aggregate.T, preferred_element_type=jnp.float32).astype(jnp.bfloat16))
    every = widen(jnp.stack(predictions))
    truth = widen(target)
    grads = []
    for member in range(MEMBERS):
        slope_sum = jnp.zeros((V, GRID), jnp.float32)
        for other in range(MEMBERS):
            slope_sum = slope_sum + smooth_slope(every[member] - every[other])
        dpred = (area[None, :] * (smooth_slope(every[member] - truth) - slope_sum / (MEMBERS - 1))).astype(jnp.bfloat16)
        dagg = jnp.dot(dpred.T, w_decode, preferred_element_type=jnp.float32)
        dout = jnp.zeros((LAT, D), jnp.float32)
        for slot in range(KD):
            dout = dout.at[decoder_src[:, slot]].add(edge_weight[:, slot, None] * dagg)
        grads.append(member_backward(latent[member], dout, outputs_saved[member], w_query, w_key, w_value, w_out))
    return jnp.stack(grads)
```

```python
import jax
import jax.numpy as jnp
from jax import lax
from jax.experimental import pallas as pl
from jax.experimental.pallas import tpu as pltpu
from jax.sharding import PartitionSpec as P

HEADS = 8
DH = 64
PAIRS = HEADS // 2
KW = 32
KD = 3
V = 100
VP = 128
EDGE = 64
OWN = 128
D = 1024
E = HEADS * DH
G = 512
MEMBERS = 8
SHARDS = 64

score_scale = 6.0
eps_norm = 1e-06
delta_smooth = 0.1

MESH = pl.DeviceIdType.MESH
f32 = jnp.float32
bf16 = jnp.bfloat16


def dot(a, b):
    return jnp.dot(a, b, preferred_element_type=f32)


def dot_t(a, b):
    return lax.dot_general(a, b, (((1,), (1,)), ((), ())), preferred_element_type=f32)


def smooth_slope(difference):
    return difference * lax.rsqrt(difference * difference + delta_smooth * delta_smooth)


def head_ones():
    row = lax.broadcasted_iota(jnp.int32, (128, 128), 0) < DH
    lane = lax.broadcasted_iota(jnp.int32, (128, 128), 1) < DH
    return jnp.where(row == lane, 1.0, 0.0).astype(bf16)


def head_means(values, ones):
    low = values.astype(bf16)
    parts = [dot(low[:, 128 * p : 128 * (p + 1)], ones) for p in range(PAIRS)]
    return jnp.concatenate(parts, axis=1) * (1.0 / DH)


def normalize(projected, ones):
    factor = lax.rsqrt(head_means(projected * projected, ones) + eps_norm)
    return projected * factor, factor


def norm_backward(grad_hat, unit_rows, factor, ones):
    return factor * (grad_hat - unit_rows * head_means(grad_hat * unit_rows, ones))


def kernel(
    latent, w_query, w_key, w_value, w_out, w_decode, window, source, edge_weight, target, area,
    out,
    x, xh, wq, wk, wv, wo, wd_raw, wd, win, src, ew, tgt, area_row,
    q_hat, q_factor, k_hat, k_factor, q_low, key_pair, value_pair,
    weight, weight_t, counts2, counts_t, count_send, count_recv, numden, mixed, mixed_halo, inverse,
    pred_rows, spread, gather, truth, fold, base, sums, sums_low, from_left, from_right,
    local_sem, halo_send, halo_recv, member_send, member_recv,
):
    m = lax.axis_index("member")
    s = lax.axis_index("space")
    has_left = s > 0
    has_right = s < SHARDS - 1
    left = (m, lax.rem(s + SHARDS - 1, SHARDS))
    right = (m, lax.rem(s + 1, SHARDS))
    peers = [(lax.rem(m + d, MEMBERS), s) for d in range(MEMBERS)]

    barrier = pltpu.get_barrier_semaphore()

    @pl.when(has_left)
    def _():
        pl.semaphore_signal(barrier, inc=1, device_id=left, device_id_type=MESH)

    @pl.when(has_right)
    def _():
        pl.semaphore_signal(barrier, inc=1, device_id=right, device_id_type=MESH)

    for d in range(1, MEMBERS):
        pl.semaphore_signal(barrier, inc=1, device_id=peers[d], device_id_type=MESH)

    pairs = [
        (latent.at[0], x), (window, win), (w_decode, wd_raw), (w_key, wk), (w_value, wv),
        (w_query, wq), (w_out, wo), (source, src), (edge_weight, ew), (target, tgt),
        (area, area_row),
    ]
    loads = [pltpu.make_async_copy(a, b, local_sem.at[i]) for i, (a, b) in enumerate(pairs)]
    for load in loads:
        load.start()
    (x_load, win_load, wd_load, wk_load, wv_load, wq_load, wo_load, src_load, ew_load, tgt_load,
     area_load) = loads

    @pl.when(jnp.logical_not(has_left))
    def _():
        xh[EDGE:] = jnp.zeros((EDGE, D), bf16)
        count_recv[:EDGE] = jnp.zeros((EDGE, OWN), bf16)
        pred_rows[OWN + EDGE :, :VP] = jnp.zeros((EDGE, VP), bf16)
        mixed_halo[EDGE:] = jnp.zeros((EDGE, E + 128), bf16)
        from_left[...] = jnp.zeros((2 * EDGE, VP), bf16)

    @pl.when(jnp.logical_not(has_right))
    def _():
        xh[:EDGE] = jnp.zeros((EDGE, D), bf16)
        count_recv[EDGE:] = jnp.zeros((EDGE, OWN), bf16)
        pred_rows[OWN : OWN + EDGE, :VP] = jnp.zeros((EDGE, VP), bf16)
        mixed_halo[:EDGE] = jnp.zeros((EDGE, E + 128), bf16)
        from_right[...] = jnp.zeros((2 * EDGE, VP), bf16)

    def halo(index, to_left, to_right):
        copies = [
            pltpu.make_async_remote_copy(
                src_ref=a, dst_ref=b, send_sem=halo_send.at[index, side],
                recv_sem=halo_recv.at[index, side], device_id=device, device_id_type=MESH,
            )
            for side, (a, b), device in ((0, to_left, left), (1, to_right, right))
        ]

        def start():
            @pl.when(has_left)
            def _():
                copies[0].start()

            @pl.when(has_right)
            def _():
                copies[1].start()

        def arrive():
            @pl.when(has_right)
            def _():
                copies[0].wait_recv()

            @pl.when(has_left)
            def _():
                copies[1].wait_recv()

        def leave():
            @pl.when(has_left)
            def _():
                copies[0].wait_send()

            @pl.when(has_right)
            def _():
                copies[1].wait_send()

        return start, arrive, leave

    def member_copies(index, rows):
        return [
            pltpu.make_async_remote_copy(
                src_ref=pred_rows.at[rows, pl.ds(0, VP)],
                dst_ref=pred_rows.at[rows, pl.ds(VP * d, VP)],
                send_sem=member_send.at[index, d],
                recv_sem=member_recv.at[index, d],
                device_id=peers[d],
                device_id_type=MESH,
            )
            for d in range(1, MEMBERS)
        ]

    lower, upper = pl.ds(0, EDGE), pl.ds(EDGE, EDGE)
    latent_halo = halo(0, (x.at[lower], xh.at[lower]), (x.at[upper], xh.at[upper]))
    count_halo = halo(
        1, (count_send.at[upper], count_recv.at[upper]), (count_send.at[lower], count_recv.at[lower])
    )
    pred_halo = halo(
        2,
        (pred_rows.at[lower, pl.ds(0, VP)], pred_rows.at[pl.ds(OWN, EDGE), pl.ds(0, VP)]),
        (pred_rows.at[upper, pl.ds(0, VP)], pred_rows.at[pl.ds(OWN + EDGE, EDGE), pl.ds(0, VP)]),
    )
    mixed_exchange = halo(
        3, (mixed.at[lower], mixed_halo.at[lower]), (mixed.at[upper], mixed_halo.at[upper])
    )
    sum_exchange = halo(
        4,
        (sums_low.at[pl.ds(OWN + EDGE, 2 * EDGE)], from_right),
        (sums_low.at[pl.ds(EDGE, 2 * EDGE)], from_left),
    )

    x_load.wait()
    one = jnp.int32(1)
    pl.semaphore_wait(
        barrier, MEMBERS - 1 + jnp.minimum(s, one) + jnp.minimum(SHARDS - 1 - s, one)
    )

    latent_halo[0]()

    ones = head_ones()
    lane = lax.broadcasted_iota(jnp.int32, (128, 128), 1)
    first_head = lane < DH
    first_ones = jnp.where(first_head, 1.0, 0.0).astype(bf16)
    second_ones = jnp.where(first_head, 0.0, 1.0).astype(bf16)

    win_load.wait()
    near = jnp.bitwise_and(win[...] - s * OWN, 255)
    place = lax.broadcasted_iota(jnp.int32, (256, 128), 0)
    turned = jnp.zeros((256, OWN), f32)
    for k in range(KW):
        turned = turned + jnp.where(near[k : k + 1] == place, 1.0, 0.0)
    counts = turned.T
    count_send[...] = turned[OWN:].astype(bf16)
    count_halo[0]()
    own_counts, halo_counts = counts[:, :OWN], counts[:, OWN:]
    counts2[...] = jnp.concatenate([own_counts, own_counts, halo_counts, halo_counts], axis=1)
    counts_t[...] = turned[:OWN]

    def split_pair(values):
        return jnp.concatenate(
            [jnp.where(first_head, values, 0.0), jnp.where(first_head, 0.0, values)], axis=0
        ).astype(bf16)

    def put_keys(rows, where, keep):
        k_unit, k_scale = normalize(dot(rows, wk[...]), ones)
        values = dot(rows, wv[...])
        if keep:
            k_hat[...] = k_unit
            k_factor[...] = k_scale
        for p in range(PAIRS):
            cols = slice(128 * p, 128 * (p + 1))
            key_pair[p, where : where + 256] = split_pair(k_unit[:, cols])
            value_pair[p, where : where + 256, :128] = split_pair(values[:, cols])
            value_pair[p, where : where + 128, 128:] = first_ones
            value_pair[p, where + 128 : where + 256, 128:] = second_ones

    def put_queries(rows, where, keep):
        q_unit, q_scale = normalize(dot(rows, wq[...]), ones)
        if keep:
            q_hat[...] = q_unit
            q_factor[...] = q_scale
        q_low[where : where + OWN] = (q_unit * (score_scale / DH)).astype(bf16)

    own_rows = x[...]
    wk_load.wait()
    wv_load.wait()
    put_keys(own_rows, 0, True)
    wq_load.wait()
    put_queries(own_rows, 0, True)

    def attend(p, where):
        cols = slice(128 * p, 128 * (p + 1))
        scores = dot_t(q_low[:OWN, cols], key_pair[p, where : where + 256])
        chosen = (counts2[:, where : where + 256] * jnp.exp(scores)).astype(bf16)
        weight[p, :, where : where + 256] = chosen
        return dot(chosen, value_pair[p, where : where + 256])

    def attend_turned(p, where, count_turned):
        cols = slice(128 * p, 128 * (p + 1))
        scores = dot_t(key_pair[p, :256], q_low[where : where + OWN, cols])
        twice = jnp.concatenate([count_turned, count_turned], axis=0)
        weight_t[p, :, where : where + OWN] = (twice * jnp.exp(scores)).astype(bf16)

    for p in range(PAIRS):
        numden[p] = attend(p, 0)

    wd_load.wait()
    wd[...] = jnp.zeros((VP, D), bf16)
    wd[:V] = wd_raw[...]
    base[...] = dot_t(own_rows, wd[...])
    wo_load.wait()
    fold[...] = dot_t(wd[...], wo[...]).astype(bf16)

    src_load.wait()
    ew_load.wait()
    area_load.wait()
    tgt_load.wait()
    for g in range(0, G, 128):
        near = jnp.bitwise_and(src[:, g : g + 128] - s * OWN, 255)
        edges = jnp.zeros((256, 128), f32)
        for k in range(KD):
            edges = edges + jnp.where(near[k : k + 1] == place, ew[k : k + 1, g : g + 128], 0.0)
        gather[g : g + 128] = edges.T.astype(bf16)
        spread[:, g : g + 128] = (edges * area_row[:, g : g + 128]).astype(bf16)
        block = tgt[:, g : g + 128].astype(f32)
        truth[g : g + 128] = jnp.concatenate([block, jnp.zeros((VP - V, 128), f32)], axis=0).T

    for p in range(PAIRS):
        attend_turned(p, 0, counts_t[...])

    latent_halo[1]()
    halo_rows = xh[...]
    put_keys(halo_rows, 256, False)
    compact = jnp.zeros((OWN, 128), f32)
    for p in range(PAIRS):
        cols = slice(128 * p, 128 * (p + 1))
        both = numden[p] + attend(p, 256)
        recip = 1.0 / both[:, 128:]
        inverse[:, cols] = recip
        mixed[:, cols] = (both[:, :128] * recip).astype(bf16)
        compact = jnp.where(jnp.bitwise_and(lane, DH - 1) == p, recip, compact)
    mixed[:, E:] = compact.astype(bf16)
    pred_rows[:OWN, :VP] = (base[...] + dot_t(mixed[:, :E], fold[...])).astype(bf16)
    pred_halo[0]()
    own_out = member_copies(0, pl.ds(0, OWN))
    for copy in own_out:
        copy.start()
    mixed_exchange[0]()

    put_queries(halo_rows, OWN, False)
    count_halo[1]()
    for p in range(PAIRS):
        attend_turned(p, OWN, count_recv[...].astype(f32))

    pred_halo[1]()
    halo_out = member_copies(1, pl.ds(OWN, OWN))
    for copy in halo_out:
        copy.start()
    for copy in own_out:
        copy.wait_recv()
    for copy in halo_out:
        copy.wait_recv()

    total = jnp.zeros((256, VP), f32)
    for g in range(0, G, 128):
        rows = gather[g : g + 128]
        mine = dot(rows, pred_rows[:, :VP])
        slopes = jnp.zeros((128, VP), f32)
        for d in range(1, MEMBERS):
            slopes = slopes + smooth_slope(mine - dot(rows, pred_rows[:, VP * d : VP * (d + 1)]))
        dpred = smooth_slope(mine - truth[g : g + 128]) - slopes * (1.0 / (MEMBERS - 1))
        total = total + dot(spread[:, g : g + 128], dpred.astype(bf16))
    sums[...] = total
    sums_low[:256] = total.astype(bf16)
    sums_low[256:] = total[:EDGE].astype(bf16)
    sum_exchange[0]()

    mixed_exchange[1]()
    lower_lane = lax.broadcasted_iota(jnp.int32, (128, 128), 0)
    inverse_halo = []
    for p in range(PAIRS):
        pick = jnp.where(lower_lane == jnp.where(first_head, p, p + DH), 1.0, 0.0).astype(bf16)
        inverse_halo.append(dot(mixed_halo[:, E:], pick))

    sum_exchange[1]()
    near_left = from_left[...].astype(f32)
    near_right = from_right[...].astype(f32)
    own_sum = (
        sums[:OWN] + jnp.concatenate([near_left[EDGE:], near_right[:EDGE]], axis=0)
    ).astype(bf16)
    halo_sum = (
        sums[OWN:] + jnp.concatenate([near_right[EDGE:], near_left[:EDGE]], axis=0)
    ).astype(bf16)

    dmixed = dot(own_sum, fold[...]) * inverse[...]
    dmixed_halo = dot(halo_sum, fold[...]) * jnp.concatenate(inverse_halo, axis=1)
    dmixed_all = jnp.concatenate([dmixed, dmixed_halo], axis=0)
    mixed_all = jnp.concatenate([mixed[:, :E], mixed_halo[:, :E]], axis=0).astype(f32)
    dmixed_low = dmixed_all.astype(bf16)
    row_low = (-dmixed_all * mixed_all).astype(bf16)
    dq_parts, dk_parts, dv_parts = [], [], []
    for p in range(PAIRS):
        cols = slice(128 * p, 128 * (p + 1))
        sides = jnp.concatenate([dmixed_low[:, cols], row_low[:, cols]], axis=1)
        dscore = (weight[p].astype(f32) * dot_t(sides[:OWN], value_pair[p])).astype(bf16)
        dq_parts.append(dot(dscore, key_pair[p]) * (score_scale / DH))
        dscore_t = (weight_t[p].astype(f32) * dot_t(value_pair[p, :256], sides)).astype(bf16)
        dk = dot(dscore_t, q_low[:, cols])
        dv = dot(weight_t[p], dmixed_low[:, cols])
        dk_parts.append(jnp.where(first_head, dk[:OWN], dk[OWN:]))
        dv_parts.append(jnp.where(first_head, dv[:OWN], dv[OWN:]))
    dq = norm_backward(jnp.concatenate(dq_parts, axis=1), q_hat[...], q_factor[...], ones)
    dk = norm_backward(jnp.concatenate(dk_parts, axis=1), k_hat[...], k_factor[...], ones)
    dv = jnp.concatenate(dv_parts, axis=1)
    grad = dot(own_sum, wd[...]) + dot_t(dq.astype(bf16), wq[...])
    grad = grad + dot_t(dk.astype(bf16), wk[...])
    grad = grad + dot_t(dv.astype(bf16), wv[...])
    out[0] = grad.astype(bf16)

    for exchange in (latent_halo, count_halo, pred_halo, mixed_exchange, sum_exchange):
        exchange[2]()
    for copy in own_out + halo_out:
        copy.wait_send()


def per_device(
    latent, w_query, w_key, w_value, w_out, w_decode, window, decoder_src, edge_weight, target, area
):
    vmem = pltpu.VMEM
    hbm = pl.BlockSpec(memory_space=pltpu.HBM)
    return pl.pallas_call(
        kernel,
        out_shape=jax.ShapeDtypeStruct((1, OWN, D), bf16),
        in_specs=[hbm] * 11,
        out_specs=pl.BlockSpec(memory_space=pltpu.VMEM),
        scratch_shapes=[
            vmem((OWN, D), bf16),
            vmem((2 * EDGE, D), bf16),
            vmem((D, E), bf16),
            vmem((D, E), bf16),
            vmem((D, E), bf16),
            vmem((E, D), bf16),
            vmem((V, D), bf16),
            vmem((VP, D), bf16),
            vmem((KW, OWN), jnp.int32),
            vmem((KD, G), jnp.int32),
            vmem((KD, G), f32),
            vmem((V, G), bf16),
            vmem((1, G), f32),
            vmem((OWN, E), f32),
            vmem((OWN, E), f32),
            vmem((OWN, E), f32),
            vmem((OWN, E), f32),
            vmem((2 * OWN, E), bf16),
            vmem((PAIRS, 512, 128), bf16),
            vmem((PAIRS, 512, 256), bf16),
            vmem((PAIRS, OWN, 512), bf16),
            vmem((PAIRS, 256, 256), bf16),
            vmem((OWN, 512), f32),
            vmem((OWN, OWN), f32),
            vmem((OWN, OWN), bf16),
            vmem((OWN, OWN), bf16),
            vmem((PAIRS, OWN, 256), f32),
            vmem((OWN, E + 128), bf16),
            vmem((2 * EDGE, E + 128), bf16),
            vmem((OWN, E), f32),
            vmem((256, MEMBERS * VP), bf16),
            vmem((256, G), bf16),
            vmem((G, 256), bf16),
            vmem((G, VP), f32),
            vmem((VP, E), bf16),
            vmem((OWN, VP), f32),
            vmem((256, VP), f32),
            vmem((320, VP), bf16),
            vmem((2 * EDGE, VP), bf16),
            vmem((2 * EDGE, VP), bf16),
            pltpu.SemaphoreType.DMA((11,)),
            pltpu.SemaphoreType.DMA((5, 2)),
            pltpu.SemaphoreType.DMA((5, 2)),
            pltpu.SemaphoreType.DMA((2, MEMBERS)),
            pltpu.SemaphoreType.DMA((2, MEMBERS)),
        ],
        compiler_params=pltpu.CompilerParams(
            collective_id=0, has_side_effects=True, vmem_limit_bytes=40 << 20
        ),
    )(
        latent, w_query, w_key, w_value, w_out, w_decode, window.T, decoder_src.T, edge_weight.T,
        target, area.reshape(1, -1),
    )


def solution(mesh):
    in_specs = (
        P("member", "space", None),
        P(),
        P(),
        P(),
        P(),
        P(),
        P("space", None),
        P("space", None),
        P("space", None),
        P(None, "space"),
        P("space"),
    )
    out_specs = P("member", "space", None)
    return jax.shard_map(
        per_device, mesh=mesh, in_specs=in_specs, out_specs=out_specs, check_vma=False
    )
```

```python
import jax
import jax.numpy as jnp
from jax import lax
from jax.experimental import pallas as pl
from jax.experimental.pallas import tpu as pltpu
from jax.sharding import PartitionSpec as P

HEADS = 8
DH = 64
PAIRS = HEADS // 2
KW = 32
KD = 3
V = 100
VP = 128
EDGE = 64
OWN = 128
D = 1024
E = HEADS * DH
G = 512
MEMBERS = 8
SHARDS = 64

score_scale = 6.0
eps_norm = 1e-06
delta_smooth = 0.1

MESH = pl.DeviceIdType.MESH
f32 = jnp.float32
bf16 = jnp.bfloat16


def dot(a, b):
    return jnp.dot(a, b, preferred_element_type=f32)


def dot_t(a, b):
    return lax.dot_general(a, b, (((1,), (1,)), ((), ())), preferred_element_type=f32)


def smooth_slope(difference):
    return difference * lax.rsqrt(difference * difference + delta_smooth * delta_smooth)


def head_ones():
    row = lax.broadcasted_iota(jnp.int32, (128, 128), 0) < DH
    lane = lax.broadcasted_iota(jnp.int32, (128, 128), 1) < DH
    return jnp.where(row == lane, 1.0, 0.0).astype(bf16)


def head_means(values, ones):
    low = values.astype(bf16)
    parts = [dot(low[:, 128 * p : 128 * (p + 1)], ones) for p in range(PAIRS)]
    return jnp.concatenate(parts, axis=1) * (1.0 / DH)


def normalize(projected, ones):
    factor = lax.rsqrt(head_means(projected * projected, ones) + eps_norm)
    return projected * factor, factor


def norm_backward(grad_hat, unit_rows, factor, ones):
    return factor * (grad_hat - unit_rows * head_means(grad_hat * unit_rows, ones))


def kernel(
    latent, w_query, w_key, w_value, w_out, w_decode, window, source, edge_weight, target, area,
    out,
    x, xh, wq, wk, wv, wo, wd_raw, wd, win, src, ew, tgt, area_row,
    q_hat, q_factor, k_hat, k_factor, q_low, key_pair, value_pair,
    weight, weight_t, counts2, counts_t, count_send, count_recv, numden, mixed, mixed_halo, inverse,
    pred_rows, spread, gather, truth, fold, base, sums, sums_low, from_left, from_right,
    local_sem, halo_send, halo_recv, member_send, member_recv,
):
    m = lax.axis_index("member")
    s = lax.axis_index("space")
    has_left = s > 0
    has_right = s < SHARDS - 1
    left = (m, lax.rem(s + SHARDS - 1, SHARDS))
    right = (m, lax.rem(s + 1, SHARDS))
    peers = [(lax.rem(m + d, MEMBERS), s) for d in range(MEMBERS)]

    barrier = pltpu.get_barrier_semaphore()

    @pl.when(has_left)
    def _():
        pl.semaphore_signal(barrier, inc=1, device_id=left, device_id_type=MESH)

    @pl.when(has_right)
    def _():
        pl.semaphore_signal(barrier, inc=1, device_id=right, device_id_type=MESH)

    for d in range(1, MEMBERS):
        pl.semaphore_signal(barrier, inc=1, device_id=peers[d], device_id_type=MESH)

    pairs = [
        (latent.at[0], x), (window, win), (w_decode, wd_raw), (w_key, wk), (w_value, wv),
        (w_query, wq), (w_out, wo), (source, src), (edge_weight, ew), (target, tgt),
        (area, area_row),
    ]
    loads = [pltpu.make_async_copy(a, b, local_sem.at[i]) for i, (a, b) in enumerate(pairs)]
    for load in loads:
        load.start()
    (x_load, win_load, wd_load, wk_load, wv_load, wq_load, wo_load, src_load, ew_load, tgt_load,
     area_load) = loads

    @pl.when(jnp.logical_not(has_left))
    def _():
        xh[EDGE:] = jnp.zeros((EDGE, D), bf16)
        count_recv[:EDGE] = jnp.zeros((EDGE, OWN), bf16)
        pred_rows[OWN + EDGE :, :VP] = jnp.zeros((EDGE, VP), bf16)
        mixed_halo[EDGE:] = jnp.zeros((EDGE, E + 128), bf16)
        from_left[...] = jnp.zeros((2 * EDGE, VP), bf16)

    @pl.when(jnp.logical_not(has_right))
    def _():
        xh[:EDGE] = jnp.zeros((EDGE, D), bf16)
        count_recv[EDGE:] = jnp.zeros((EDGE, OWN), bf16)
        pred_rows[OWN : OWN + EDGE, :VP] = jnp.zeros((EDGE, VP), bf16)
        mixed_halo[:EDGE] = jnp.zeros((EDGE, E + 128), bf16)
        from_right[...] = jnp.zeros((2 * EDGE, VP), bf16)

    def halo(index, to_left, to_right):
        copies = [
            pltpu.make_async_remote_copy(
                src_ref=a, dst_ref=b, send_sem=halo_send.at[index, side],
                recv_sem=halo_recv.at[index, side], device_id=device, device_id_type=MESH,
            )
            for side, (a, b), device in ((0, to_left, left), (1, to_right, right))
        ]

        def start():
            @pl.when(has_left)
            def _():
                copies[0].start()

            @pl.when(has_right)
            def _():
                copies[1].start()

        def arrive():
            @pl.when(has_right)
            def _():
                copies[0].wait_recv()

            @pl.when(has_left)
            def _():
                copies[1].wait_recv()

        def leave():
            @pl.when(has_left)
            def _():
                copies[0].wait_send()

            @pl.when(has_right)
            def _():
                copies[1].wait_send()

        return start, arrive, leave

    def member_copies(index, rows):
        return [
            pltpu.make_async_remote_copy(
                src_ref=pred_rows.at[rows, pl.ds(0, VP)],
                dst_ref=pred_rows.at[rows, pl.ds(VP * d, VP)],
                send_sem=member_send.at[index, d],
                recv_sem=member_recv.at[index, d],
                device_id=peers[d],
                device_id_type=MESH,
            )
            for d in range(1, MEMBERS)
        ]

    lower, upper = pl.ds(0, EDGE), pl.ds(EDGE, EDGE)
    latent_halo = halo(0, (x.at[lower], xh.at[lower]), (x.at[upper], xh.at[upper]))
    count_halo = halo(
        1, (count_send.at[upper], count_recv.at[upper]), (count_send.at[lower], count_recv.at[lower])
    )
    pred_halo = halo(
        2,
        (pred_rows.at[lower, pl.ds(0, VP)], pred_rows.at[pl.ds(OWN, EDGE), pl.ds(0, VP)]),
        (pred_rows.at[upper, pl.ds(0, VP)], pred_rows.at[pl.ds(OWN + EDGE, EDGE), pl.ds(0, VP)]),
    )
    mixed_exchange = halo(
        3, (mixed.at[lower], mixed_halo.at[lower]), (mixed.at[upper], mixed_halo.at[upper])
    )
    sum_exchange = halo(
        4,
        (sums_low.at[pl.ds(OWN + EDGE, 2 * EDGE)], from_right),
        (sums_low.at[pl.ds(EDGE, 2 * EDGE)], from_left),
    )

    x_load.wait()
    one = jnp.int32(1)
    pl.semaphore_wait(
        barrier, MEMBERS - 1 + jnp.minimum(s, one) + jnp.minimum(SHARDS - 1 - s, one)
    )

    latent_halo[0]()

    ones = head_ones()
    lane = lax.broadcasted_iota(jnp.int32, (128, 128), 1)
    first_head = lane < DH
    first_ones = jnp.where(first_head, 1.0, 0.0).astype(bf16)
    second_ones = jnp.where(first_head, 0.0, 1.0).astype(bf16)

    win_load.wait()
    near = jnp.bitwise_and(win[...] - s * OWN, 255)
    place = lax.broadcasted_iota(jnp.int32, (256, 128), 0)
    turned = jnp.zeros((256, OWN), f32)
    for k in range(KW):
        turned = turned + jnp.where(near[k : k + 1] == place, 1.0, 0.0)
    counts = turned.T
    count_send[...] = turned[OWN:].astype(bf16)
    count_halo[0]()
    own_counts, halo_counts = counts[:, :OWN], counts[:, OWN:]
    counts2[...] = jnp.concatenate([own_counts, own_counts, halo_counts, halo_counts], axis=1)
    counts_t[...] = turned[:OWN]

    def split_pair(values):
        return jnp.concatenate(
            [jnp.where(first_head, values, 0.0), jnp.where(first_head, 0.0, values)], axis=0
        ).astype(bf16)

    def put_keys(rows, where, keep):
        k_unit, k_scale = normalize(dot(rows, wk[...]), ones)
        values = dot(rows, wv[...])
        if keep:
            k_hat[...] = k_unit
            k_factor[...] = k_scale
        for p in range(PAIRS):
            cols = slice(128 * p, 128 * (p + 1))
            key_pair[p, where : where + 256] = split_pair(k_unit[:, cols])
            value_pair[p, where : where + 256, :128] = split_pair(values[:, cols])
            value_pair[p, where : where + 128, 128:] = first_ones
            value_pair[p, where + 128 : where + 256, 128:] = second_ones

    def put_queries(rows, where, keep):
        q_unit, q_scale = normalize(dot(rows, wq[...]), ones)
        if keep:
            q_hat[...] = q_unit
            q_factor[...] = q_scale
        q_low[where : where + OWN] = (q_unit * (score_scale / DH)).astype(bf16)

    own_rows = x[...]
    wk_load.wait()
    wv_load.wait()
    put_keys(own_rows, 0, True)
    wq_load.wait()
    put_queries(own_rows, 0, True)

    def attend(p, where):
        cols = slice(128 * p, 128 * (p + 1))
        scores = dot_t(q_low[:OWN, cols], key_pair[p, where : where + 256])
        chosen = (counts2[:, where : where + 256] * jnp.exp(scores)).astype(bf16)
        weight[p, :, where : where + 256] = chosen
        return dot(chosen, value_pair[p, where : where + 256])

    def attend_turned(p, where, count_turned):
        cols = slice(128 * p, 128 * (p + 1))
        scores = dot_t(key_pair[p, :256], q_low[where : where + OWN, cols])
        twice = jnp.concatenate([count_turned, count_turned], axis=0)
        weight_t[p, :, where : where + OWN] = (twice * jnp.exp(scores)).astype(bf16)

    for p in range(PAIRS):
        numden[p] = attend(p, 0)

    wd_load.wait()
    wd[...] = jnp.zeros((VP, D), bf16)
    wd[:V] = wd_raw[...]
    base[...] = dot_t(own_rows, wd[...])
    wo_load.wait()
    fold[...] = dot_t(wd[...], wo[...]).astype(bf16)

    src_load.wait()
    ew_load.wait()
    area_load.wait()
    tgt_load.wait()
    for g in range(0, G, 128):
        near = jnp.bitwise_and(src[:, g : g + 128] - s * OWN, 255)
        edges = jnp.zeros((256, 128), f32)
        for k in range(KD):
            edges = edges + jnp.where(near[k : k + 1] == place, ew[k : k + 1, g : g + 128], 0.0)
        gather[g : g + 128] = edges.T.astype(bf16)
        spread[:, g : g + 128] = (edges * area_row[:, g : g + 128]).astype(bf16)
        block = tgt[:, g : g + 128].astype(f32)
        truth[g : g + 128] = jnp.concatenate([block, jnp.zeros((VP - V, 128), f32)], axis=0).T

    for p in range(PAIRS):
        attend_turned(p, 0, counts_t[...])

    latent_halo[1]()
    halo_rows = xh[...]
    put_keys(halo_rows, 256, False)
    compact = jnp.zeros((OWN, 128), f32)
    for p in range(PAIRS):
        cols = slice(128 * p, 128 * (p + 1))
        both = numden[p] + attend(p, 256)
        recip = 1.0 / both[:, 128:]
        inverse[:, cols] = recip
        mixed[:, cols] = (both[:, :128] * recip).astype(bf16)
        compact = jnp.where(jnp.bitwise_and(lane, DH - 1) == p, recip, compact)
    mixed[:, E:] = compact.astype(bf16)
    pred_rows[:OWN, :VP] = (base[...] + dot_t(mixed[:, :E], fold[...])).astype(bf16)
    pred_halo[0]()
    own_out = member_copies(0, pl.ds(0, OWN))
    for copy in own_out:
        copy.start()
    mixed_exchange[0]()

    put_queries(halo_rows, OWN, False)
    count_halo[1]()
    for p in range(PAIRS):
        attend_turned(p, OWN, count_recv[...].astype(f32))

    pred_halo[1]()
    halo_out = member_copies(1, pl.ds(OWN, OWN))
    for copy in halo_out:
        copy.start()
    for copy in own_out:
        copy.wait_recv()
    for copy in halo_out:
        copy.wait_recv()

    total = jnp.zeros((256, VP), f32)
    for g in range(0, G, 128):
        rows = gather[g : g + 128]
        mine = dot(rows, pred_rows[:, :VP])
        slopes = jnp.zeros((128, VP), f32)
        for d in range(1, MEMBERS):
            slopes = slopes + smooth_slope(mine - dot(rows, pred_rows[:, VP * d : VP * (d + 1)]))
        dpred = smooth_slope(mine - truth[g : g + 128]) - slopes * (1.0 / (MEMBERS - 1))
        total = total + dot(spread[:, g : g + 128], dpred.astype(bf16))
    sums[...] = total
    sums_low[:256] = total.astype(bf16)
    sums_low[256:] = total[:EDGE].astype(bf16)
    sum_exchange[0]()

    mixed_exchange[1]()
    lower_lane = lax.broadcasted_iota(jnp.int32, (128, 128), 0)
    inverse_halo = []
    for p in range(PAIRS):
        pick = jnp.where(lower_lane == jnp.where(first_head, p, p + DH), 1.0, 0.0).astype(bf16)
        inverse_halo.append(dot(mixed_halo[:, E:], pick))

    sum_exchange[1]()
    near_left = from_left[...].astype(f32)
    near_right = from_right[...].astype(f32)
    own_sum = (
        sums[:OWN] + jnp.concatenate([near_left[EDGE:], near_right[:EDGE]], axis=0)
    ).astype(bf16)
    halo_sum = (
        sums[OWN:] + jnp.concatenate([near_right[EDGE:], near_left[:EDGE]], axis=0)
    ).astype(bf16)

    dmixed = dot(own_sum, fold[...]) * inverse[...]
    dmixed_halo = dot(halo_sum, fold[...]) * jnp.concatenate(inverse_halo, axis=1)
    dmixed_all = jnp.concatenate([dmixed, dmixed_halo], axis=0)
    mixed_all = jnp.concatenate([mixed[:, :E], mixed_halo[:, :E]], axis=0).astype(f32)
    dmixed_low = dmixed_all.astype(bf16)
    row_low = (-dmixed_all * mixed_all).astype(bf16)
    dq_parts, dk_parts, dv_parts = [], [], []
    for p in range(PAIRS):
        cols = slice(128 * p, 128 * (p + 1))
        sides = jnp.concatenate([dmixed_low[:, cols], row_low[:, cols]], axis=1)
        dscore = (weight[p].astype(f32) * dot_t(sides[:OWN], value_pair[p])).astype(bf16)
        dq_parts.append(dot(dscore, key_pair[p]) * (score_scale / DH))
        dscore_t = (weight_t[p].astype(f32) * dot_t(value_pair[p, :256], sides)).astype(bf16)
        dk = dot(dscore_t, q_low[:, cols])
        dv = dot(weight_t[p], dmixed_low[:, cols])
        dk_parts.append(jnp.where(first_head, dk[:OWN], dk[OWN:]))
        dv_parts.append(jnp.where(first_head, dv[:OWN], dv[OWN:]))
    dq = norm_backward(jnp.concatenate(dq_parts, axis=1), q_hat[...], q_factor[...], ones)
    dk = norm_backward(jnp.concatenate(dk_parts, axis=1), k_hat[...], k_factor[...], ones)
    dv = jnp.concatenate(dv_parts, axis=1)
    grad = dot(own_sum, wd[...]) + dot_t(dq.astype(bf16), wq[...])
    grad = grad + dot_t(dk.astype(bf16), wk[...])
    grad = grad + dot_t(dv.astype(bf16), wv[...])
    out[0] = grad.astype(bf16)

    for exchange in (latent_halo, count_halo, pred_halo, mixed_exchange, sum_exchange):
        exchange[2]()
    for copy in own_out + halo_out:
        copy.wait_send()


def per_device(
    latent, w_query, w_key, w_value, w_out, w_decode, window, decoder_src, edge_weight, target, area
):
    vmem = pltpu.VMEM
    hbm = pl.BlockSpec(memory_space=pltpu.HBM)
    return pl.pallas_call(
        kernel,
        out_shape=jax.ShapeDtypeStruct((1, OWN, D), bf16),
        in_specs=[hbm] * 11,
        out_specs=pl.BlockSpec(memory_space=pltpu.VMEM),
        scratch_shapes=[
            vmem((OWN, D), bf16),
            vmem((2 * EDGE, D), bf16),
            vmem((D, E), bf16),
            vmem((D, E), bf16),
            vmem((D, E), bf16),
            vmem((E, D), bf16),
            vmem((V, D), bf16),
            vmem((VP, D), bf16),
            vmem((KW, OWN), jnp.int32),
            vmem((KD, G), jnp.int32),
            vmem((KD, G), f32),
            vmem((V, G), bf16),
            vmem((1, G), f32),
            vmem((OWN, E), f32),
            vmem((OWN, E), f32),
            vmem((OWN, E), f32),
            vmem((OWN, E), f32),
            vmem((2 * OWN, E), bf16),
            vmem((PAIRS, 512, 128), bf16),
            vmem((PAIRS, 512, 256), bf16),
            vmem((PAIRS, OWN, 512), bf16),
            vmem((PAIRS, 256, 256), bf16),
            vmem((OWN, 512), f32),
            vmem((OWN, OWN), f32),
            vmem((OWN, OWN), bf16),
            vmem((OWN, OWN), bf16),
            vmem((PAIRS, OWN, 256), f32),
            vmem((OWN, E + 128), bf16),
            vmem((2 * EDGE, E + 128), bf16),
            vmem((OWN, E), f32),
            vmem((256, MEMBERS * VP), bf16),
            vmem((256, G), bf16),
            vmem((G, 256), bf16),
            vmem((G, VP), f32),
            vmem((VP, E), bf16),
            vmem((OWN, VP), f32),
            vmem((256, VP), f32),
            vmem((320, VP), bf16),
            vmem((2 * EDGE, VP), bf16),
            vmem((2 * EDGE, VP), bf16),
            pltpu.SemaphoreType.DMA((11,)),
            pltpu.SemaphoreType.DMA((5, 2)),
            pltpu.SemaphoreType.DMA((5, 2)),
            pltpu.SemaphoreType.DMA((2, MEMBERS)),
            pltpu.SemaphoreType.DMA((2, MEMBERS)),
        ],
        compiler_params=pltpu.CompilerParams(
            collective_id=0, has_side_effects=True, vmem_limit_bytes=60 << 20
        ),
    )(
        latent, w_query, w_key, w_value, w_out, w_decode, window.T, decoder_src.T, edge_weight.T,
        target, area.reshape(1, -1),
    )


def solution(mesh):
    in_specs = (
        P("member", "space", None),
        P(),
        P(),
        P(),
        P(),
        P(),
        P("space", None),
        P("space", None),
        P("space", None),
        P(None, "space"),
        P("space"),
    )
    out_specs = P("member", "space", None)
    return jax.shard_map(
        per_device, mesh=mesh, in_specs=in_specs, out_specs=out_specs, check_vma=False
    )
```

```python
import jax
import jax.numpy as jnp
from jax import lax
from jax.experimental import pallas as pl
from jax.experimental.pallas import tpu as pltpu
from jax.sharding import PartitionSpec as P

HEADS = 8
DH = 64
PAIRS = HEADS // 2
KW = 32
KD = 3
V = 100
VP = 128
FIRST, SECOND = 112, 120
EDGE = 64
OWN = 128
D = 1024
E = HEADS * DH
G = 512
MEMBERS = 8
SHARDS = 64

score_scale = 6.0
eps_norm = 1e-06
delta_smooth = 0.1

MESH = pl.DeviceIdType.MESH
f32 = jnp.float32
bf16 = jnp.bfloat16


def dot(a, b):
    return jnp.dot(a, b, preferred_element_type=f32)


def dot_t(a, b):
    return lax.dot_general(a, b, (((1,), (1,)), ((), ())), preferred_element_type=f32)


def smooth_slope(difference):
    return difference * lax.rsqrt(difference * difference + delta_smooth * delta_smooth)


def head_ones():
    row = lax.broadcasted_iota(jnp.int32, (128, 128), 0) < DH
    lane = lax.broadcasted_iota(jnp.int32, (128, 128), 1) < DH
    return jnp.where(row == lane, 1.0, 0.0).astype(bf16)


def head_means(values, ones):
    low = values.astype(bf16)
    parts = [dot(low[:, 128 * p : 128 * (p + 1)], ones) for p in range(PAIRS)]
    return jnp.concatenate(parts, axis=1) * (1.0 / DH)


def normalize(projected, ones):
    factor = lax.rsqrt(head_means(projected * projected, ones) + eps_norm)
    return projected * factor, factor


def norm_backward(grad_hat, unit_rows, factor, ones):
    return factor * (grad_hat - unit_rows * head_means(grad_hat * unit_rows, ones))


def kernel(
    latent, w_query, w_key, w_value, w_out, w_decode, window, source, edge_weight, target, area,
    out,
    x, xh, wq, wk, wv, wo, wd_raw, wd, win, src, ew, tgt, area_row,
    q_hat, q_factor, k_hat, k_factor, q_low, key_pair, value_pair,
    weight, weight_t, counts2, counts_t, count_send, count_recv, numden, early, early_halo, mixed, mixed_halo, inverse, inverse_halo, numerator_halo,
    pred_rows, spread, gather, truth, fold, base, sums, sums_low, from_left, from_right,
    local_sem, halo_send, halo_recv, member_send, member_recv,
):
    m = lax.axis_index("member")
    s = lax.axis_index("space")
    has_left = s > 0
    has_right = s < SHARDS - 1
    left = (m, lax.rem(s + SHARDS - 1, SHARDS))
    right = (m, lax.rem(s + 1, SHARDS))
    core = lax.rem(m, 2)
    peers = [
        (lax.rem(m - core + d // 2 * 2, MEMBERS) + (core if d % 2 == 0 else 1 - core), s)
        for d in range(MEMBERS)
    ]

    barrier = pltpu.get_barrier_semaphore()

    @pl.when(has_left)
    def _():
        pl.semaphore_signal(barrier, inc=1, device_id=left, device_id_type=MESH)

    @pl.when(has_right)
    def _():
        pl.semaphore_signal(barrier, inc=1, device_id=right, device_id_type=MESH)

    for d in range(1, MEMBERS):
        pl.semaphore_signal(barrier, inc=1, device_id=peers[d], device_id_type=MESH)

    pairs = [
        (latent.at[0], x), (window, win), (w_decode, wd_raw), (w_key, wk), (w_value, wv),
        (w_query, wq), (w_out, wo), (source, src), (edge_weight, ew), (target, tgt),
        (area, area_row),
    ]
    loads = [pltpu.make_async_copy(a, b, local_sem.at[i]) for i, (a, b) in enumerate(pairs)]
    for load in loads:
        load.start()
    (x_load, win_load, wd_load, wk_load, wv_load, wq_load, wo_load, src_load, ew_load, tgt_load,
     area_load) = loads

    @pl.when(jnp.logical_not(has_left))
    def _():
        xh[EDGE:] = jnp.zeros((EDGE, D), bf16)
        count_recv[:EDGE] = jnp.zeros((EDGE, OWN), bf16)
        pred_rows[OWN + EDGE :, :VP] = jnp.zeros((EDGE, VP), bf16)
        early_halo[EDGE:] = jnp.zeros((EDGE, E), bf16)
        from_left[...] = jnp.zeros((2 * EDGE, VP), bf16)

    @pl.when(jnp.logical_not(has_right))
    def _():
        xh[:EDGE] = jnp.zeros((EDGE, D), bf16)
        count_recv[EDGE:] = jnp.zeros((EDGE, OWN), bf16)
        pred_rows[OWN : OWN + EDGE, :VP] = jnp.zeros((EDGE, VP), bf16)
        early_halo[:EDGE] = jnp.zeros((EDGE, E), bf16)
        from_right[...] = jnp.zeros((2 * EDGE, VP), bf16)

    def halo(index, to_left, to_right):
        copies = [
            pltpu.make_async_remote_copy(
                src_ref=a, dst_ref=b, send_sem=halo_send.at[index, side],
                recv_sem=halo_recv.at[index, side], device_id=device, device_id_type=MESH,
            )
            for side, (a, b), device in ((0, to_left, left), (1, to_right, right))
        ]

        def start():
            @pl.when(has_left)
            def _():
                copies[0].start()

            @pl.when(has_right)
            def _():
                copies[1].start()

        def arrive():
            @pl.when(has_right)
            def _():
                copies[0].wait_recv()

            @pl.when(has_left)
            def _():
                copies[1].wait_recv()

        def leave():
            @pl.when(has_left)
            def _():
                copies[0].wait_send()

            @pl.when(has_right)
            def _():
                copies[1].wait_send()

        return start, arrive, leave

    def relay_copies(index, rows):
        return [
            pltpu.make_async_remote_copy(
                src_ref=pred_rows.at[rows, pl.ds(VP * d, VP)],
                dst_ref=pred_rows.at[rows, pl.ds(VP * (d + 1), VP)],
                send_sem=member_send.at[index, d + 1],
                recv_sem=member_recv.at[index, d + 1],
                device_id=peers[1],
                device_id_type=MESH,
            )
            for d in (2, 4, 6)
        ]

    def member_copies(index, rows, slots=range(1, MEMBERS)):
        return [
            pltpu.make_async_remote_copy(
                src_ref=pred_rows.at[rows, pl.ds(0, VP)],
                dst_ref=pred_rows.at[rows, pl.ds(VP * d, VP)],
                send_sem=member_send.at[index, d],
                recv_sem=member_recv.at[index, d],
                device_id=peers[d],
                device_id_type=MESH,
            )
            for d in slots
        ]

    lower, upper = pl.ds(0, EDGE), pl.ds(EDGE, EDGE)
    latent_halo = halo(0, (x.at[lower], xh.at[lower]), (x.at[upper], xh.at[upper]))
    count_halo = halo(
        1, (count_send.at[upper], count_recv.at[upper]), (count_send.at[lower], count_recv.at[lower])
    )
    pred_halo = halo(
        2,
        (pred_rows.at[lower, pl.ds(0, VP)], pred_rows.at[pl.ds(OWN, EDGE), pl.ds(0, VP)]),
        (pred_rows.at[upper, pl.ds(0, VP)], pred_rows.at[pl.ds(OWN + EDGE, EDGE), pl.ds(0, VP)]),
    )
    early_exchange = halo(
        3, (early.at[lower], early_halo.at[lower]), (early.at[upper], early_halo.at[upper])
    )
    sum_exchange = halo(
        4,
        (sums_low.at[pl.ds(OWN + EDGE, 2 * EDGE)], from_right),
        (sums_low.at[pl.ds(EDGE, 2 * EDGE)], from_left),
    )

    x_load.wait()
    one = jnp.int32(1)
    pl.semaphore_wait(
        barrier, MEMBERS - 1 + jnp.minimum(s, one) + jnp.minimum(SHARDS - 1 - s, one)
    )

    latent_halo[0]()

    ones = head_ones()
    lane = lax.broadcasted_iota(jnp.int32, (128, 128), 1)
    first_head = lane < DH
    first_ones = jnp.where(first_head, 1.0, 0.0).astype(bf16)
    second_ones = jnp.where(first_head, 0.0, 1.0).astype(bf16)

    win_load.wait()
    near = jnp.bitwise_and(win[...] - s * OWN, 255)
    place = lax.broadcasted_iota(jnp.int32, (256, 128), 0)
    turned = jnp.zeros((256, OWN), f32)
    for k in range(KW):
        turned = turned + jnp.where(near[k : k + 1] == place, 1.0, 0.0)
    counts = turned.T
    count_send[...] = turned[OWN:].astype(bf16)
    count_halo[0]()
    own_counts, halo_counts = counts[:, :OWN], counts[:, OWN:]
    counts2[...] = jnp.concatenate([own_counts, own_counts, halo_counts, halo_counts], axis=1)
    counts_t[...] = turned[:OWN]

    def split_pair(values):
        return jnp.concatenate(
            [jnp.where(first_head, values, 0.0), jnp.where(first_head, 0.0, values)], axis=0
        ).astype(bf16)

    def put_keys(rows, where, keep):
        k_unit, k_scale = normalize(dot(rows, wk[...]), ones)
        values = dot(rows, wv[...])
        if keep:
            k_hat[...] = k_unit
            k_factor[...] = k_scale
        for p in range(PAIRS):
            cols = slice(128 * p, 128 * (p + 1))
            key_pair[p, where : where + 256] = split_pair(k_unit[:, cols])
            value_pair[p, where : where + 256, :128] = split_pair(values[:, cols])
            value_pair[p, where : where + 128, 128:] = first_ones
            value_pair[p, where + 128 : where + 256, 128:] = second_ones

    def put_queries(rows, where, keep):
        q_unit, q_scale = normalize(dot(rows, wq[...]), ones)
        if keep:
            q_hat[...] = q_unit
            q_factor[...] = q_scale
        q_low[where : where + OWN] = (q_unit * (score_scale / DH)).astype(bf16)

    own_rows = x[...]
    wk_load.wait()
    wv_load.wait()
    put_keys(own_rows, 0, True)
    wq_load.wait()
    put_queries(own_rows, 0, True)

    def attend(p, where):
        cols = slice(128 * p, 128 * (p + 1))
        scores = dot_t(q_low[:OWN, cols], key_pair[p, where : where + 256])
        chosen = (counts2[:, where : where + 256] * jnp.exp(scores)).astype(bf16)
        weight[p, :, where : where + 256] = chosen
        return dot(chosen, value_pair[p, where : where + 256])

    def attend_turned(p, where, count_turned):
        cols = slice(128 * p, 128 * (p + 1))
        scores = dot_t(key_pair[p, :256], q_low[where : where + OWN, cols])
        twice = jnp.concatenate([count_turned, count_turned], axis=0)
        weight_t[p, :, where : where + OWN] = (twice * jnp.exp(scores)).astype(bf16)

    for p in range(PAIRS):
        both = attend(p, 0)
        numden[p] = both
        early[:, 128 * p : 128 * (p + 1)] = both[:, :128].astype(bf16)

    wd_load.wait()
    wd[...] = jnp.zeros((VP, D), bf16)
    wd[:V] = wd_raw[...]
    base[...] = dot_t(own_rows, wd[...])
    wo_load.wait()
    fold[...] = dot_t(wd[...], wo[...]).astype(bf16)

    src_load.wait()
    ew_load.wait()
    area_load.wait()
    tgt_load.wait()
    for g in range(0, G, 128):
        near = jnp.bitwise_and(src[:, g : g + 128] - s * OWN, 255)
        edges = jnp.zeros((256, 128), f32)
        for k in range(KD):
            edges = edges + jnp.where(near[k : k + 1] == place, ew[k : k + 1, g : g + 128], 0.0)
        gather[g : g + 128] = edges.T.astype(bf16)
        spread[:, g : g + 128] = (edges * area_row[:, g : g + 128]).astype(bf16)
        block = tgt[:, g : g + 128].astype(f32)
        truth[g : g + 128] = jnp.concatenate([block, jnp.zeros((VP - V, 128), f32)], axis=0).T

    for p in range(PAIRS):
        attend_turned(p, 0, counts_t[...])

    latent_halo[2]()
    early_exchange[0]()

    latent_halo[1]()
    halo_rows = xh[...]
    put_keys(halo_rows, 256, False)
    decoded = base[...]
    for p in range(PAIRS):
        cols = slice(128 * p, 128 * (p + 1))
        both = numden[p] + attend(p, 256)
        recip = 1.0 / both[:, 128:]
        inverse[:, cols] = recip
        mixed[:, cols] = (both[:, :128] * recip).astype(bf16)
        decoded = jnp.where(lane == SECOND + p, recip, decoded)
        decoded = jnp.where(lane == FIRST + p, pltpu.roll(recip, DH, 1), decoded)
    pred_rows[:OWN, :VP] = (decoded + dot_t(mixed[...], fold[...])).astype(bf16)
    pred_halo[0]()
    own_out = member_copies(0, pl.ds(0, OWN), (4, 2, 6, 1))
    for copy in own_out:
        copy.start()

    put_queries(halo_rows, OWN, False)
    count_halo[1]()
    crossed = count_recv[...].astype(f32)
    for p in range(PAIRS):
        attend_turned(p, OWN, crossed)
    crossed = crossed.T
    crossed = jnp.concatenate([crossed, crossed], axis=1)
    for p in range(PAIRS):
        scores = dot_t(q_low[OWN:, 128 * p : 128 * (p + 1)], key_pair[p, :256])
        numerator_halo[p] = dot((crossed * jnp.exp(scores)).astype(bf16), value_pair[p, :256, :128])

    pred_halo[1]()
    halo_out = member_copies(1, pl.ds(OWN, OWN))
    for copy in halo_out:
        copy.start()
    for copy in own_out:
        copy.wait_recv()
    own_relay = relay_copies(0, pl.ds(0, OWN))
    for copy in own_relay:
        copy.start()
    early_exchange[1]()
    row = lax.broadcasted_iota(jnp.int32, (128, 128), 0)
    for p in range(PAIRS):
        cols = slice(128 * p, 128 * (p + 1))
        pick = jnp.where(row == jnp.where(first_head, FIRST + p, SECOND + p), 1.0, 0.0).astype(bf16)
        recip = dot(pred_rows[OWN:, :VP], pick)
        inverse_halo[:, cols] = recip
        mixed_halo[:, cols] = (
            (numerator_halo[p] + early_halo[:, cols].astype(f32)) * recip
        ).astype(bf16)
    for copy in own_relay:
        copy.wait_recv()
    for copy in halo_out:
        copy.wait_recv()

    total = jnp.zeros((256, VP), f32)
    for g in range(0, G, 128):
        rows = gather[g : g + 128]
        mine = dot(rows, pred_rows[:, :VP])
        slopes = jnp.zeros((128, VP), f32)
        for d in range(1, MEMBERS):
            slopes = slopes + smooth_slope(mine - dot(rows, pred_rows[:, VP * d : VP * (d + 1)]))
        dpred = smooth_slope(mine - truth[g : g + 128]) - slopes * (1.0 / (MEMBERS - 1))
        total = total + dot(spread[:, g : g + 128], dpred.astype(bf16))
    sums[...] = total
    sums_low[:256] = total.astype(bf16)
    sums_low[256:] = total[:EDGE].astype(bf16)
    sum_exchange[0]()

    sum_exchange[1]()
    near_left = from_left[...].astype(f32)
    near_right = from_right[...].astype(f32)
    own_sum = (
        sums[:OWN] + jnp.concatenate([near_left[EDGE:], near_right[:EDGE]], axis=0)
    ).astype(bf16)
    halo_sum = (
        sums[OWN:] + jnp.concatenate([near_right[EDGE:], near_left[:EDGE]], axis=0)
    ).astype(bf16)

    dmixed = dot(own_sum, fold[...]) * inverse[...]
    dmixed_halo = dot(halo_sum, fold[...]) * inverse_halo[...]
    dmixed_all = jnp.concatenate([dmixed, dmixed_halo], axis=0)
    mixed_all = jnp.concatenate([mixed[...], mixed_halo[...]], axis=0).astype(f32)
    dmixed_low = dmixed_all.astype(bf16)
    row_low = (-dmixed_all * mixed_all).astype(bf16)
    dq_parts, dk_parts, dv_parts = [], [], []
    for p in range(PAIRS):
        cols = slice(128 * p, 128 * (p + 1))
        sides = jnp.concatenate([dmixed_low[:, cols], row_low[:, cols]], axis=1)
        dscore = (weight[p].astype(f32) * dot_t(sides[:OWN], value_pair[p])).astype(bf16)
        dq_parts.append(dot(dscore, key_pair[p]) * (score_scale / DH))
        dscore_t = (weight_t[p].astype(f32) * dot_t(value_pair[p, :256], sides)).astype(bf16)
        dk = dot(dscore_t, q_low[:, cols])
        dv = dot(weight_t[p], dmixed_low[:, cols])
        dk_parts.append(jnp.where(first_head, dk[:OWN], dk[OWN:]))
        dv_parts.append(jnp.where(first_head, dv[:OWN], dv[OWN:]))
    dq = norm_backward(jnp.concatenate(dq_parts, axis=1), q_hat[...], q_factor[...], ones)
    dk = norm_backward(jnp.concatenate(dk_parts, axis=1), k_hat[...], k_factor[...], ones)
    dv = jnp.concatenate(dv_parts, axis=1)
    grad = dot(own_sum, wd[...]) + dot_t(dq.astype(bf16), wq[...])
    grad = grad + dot_t(dk.astype(bf16), wk[...])
    grad = grad + dot_t(dv.astype(bf16), wv[...])
    out[0] = grad.astype(bf16)

    for exchange in (count_halo, pred_halo, early_exchange, sum_exchange):
        exchange[2]()
    for copy in own_out + own_relay + halo_out:
        copy.wait_send()


def per_device(
    latent, w_query, w_key, w_value, w_out, w_decode, window, decoder_src, edge_weight, target, area
):
    vmem = pltpu.VMEM
    hbm = pl.BlockSpec(memory_space=pltpu.HBM)
    return pl.pallas_call(
        kernel,
        out_shape=jax.ShapeDtypeStruct((1, OWN, D), bf16),
        in_specs=[hbm] * 11,
        out_specs=pl.BlockSpec(memory_space=pltpu.VMEM),
        scratch_shapes=[
            vmem((OWN, D), bf16),
            vmem((2 * EDGE, D), bf16),
            vmem((D, E), bf16),
            vmem((D, E), bf16),
            vmem((D, E), bf16),
            vmem((E, D), bf16),
            vmem((V, D), bf16),
            vmem((VP, D), bf16),
            vmem((KW, OWN), jnp.int32),
            vmem((KD, G), jnp.int32),
            vmem((KD, G), f32),
            vmem((V, G), bf16),
            vmem((1, G), f32),
            vmem((OWN, E), f32),
            vmem((OWN, E), f32),
            vmem((OWN, E), f32),
            vmem((OWN, E), f32),
            vmem((2 * OWN, E), bf16),
            vmem((PAIRS, 512, 128), bf16),
            vmem((PAIRS, 512, 256), bf16),
            vmem((PAIRS, OWN, 512), bf16),
            vmem((PAIRS, 256, 256), bf16),
            vmem((OWN, 512), f32),
            vmem((OWN, OWN), f32),
            vmem((OWN, OWN), bf16),
            vmem((OWN, OWN), bf16),
            vmem((PAIRS, OWN, 256), f32),
            vmem((OWN, E), bf16),
            vmem((2 * EDGE, E), bf16),
            vmem((OWN, E), bf16),
            vmem((2 * EDGE, E), bf16),
            vmem((OWN, E), f32),
            vmem((2 * EDGE, E), f32),
            vmem((PAIRS, 2 * EDGE, 128), f32),
            vmem((256, MEMBERS * VP), bf16),
            vmem((256, G), bf16),
            vmem((G, 256), bf16),
            vmem((G, VP), f32),
            vmem((VP, E), bf16),
            vmem((OWN, VP), f32),
            vmem((256, VP), f32),
            vmem((320, VP), bf16),
            vmem((2 * EDGE, VP), bf16),
            vmem((2 * EDGE, VP), bf16),
            pltpu.SemaphoreType.DMA((11,)),
            pltpu.SemaphoreType.DMA((5, 2)),
            pltpu.SemaphoreType.DMA((5, 2)),
            pltpu.SemaphoreType.DMA((2, MEMBERS)),
            pltpu.SemaphoreType.DMA((2, MEMBERS)),
        ],
        compiler_params=pltpu.CompilerParams(
            collective_id=0, has_side_effects=True, vmem_limit_bytes=60 << 20
        ),
    )(
        latent, w_query, w_key, w_value, w_out, w_decode, window.T, decoder_src.T, edge_weight.T,
        target, area.reshape(1, -1),
    )


def solution(mesh):
    in_specs = (
        P("member", "space", None),
        P(),
        P(),
        P(),
        P(),
        P(),
        P("space", None),
        P("space", None),
        P("space", None),
        P(None, "space"),
        P("space"),
    )
    out_specs = P("member", "space", None)
    return jax.shard_map(
        per_device, mesh=mesh, in_specs=in_specs, out_specs=out_specs, check_vma=False
    )
```

```python
import jax
import jax.numpy as jnp
from jax import lax
from jax.experimental import pallas as pl
from jax.experimental.pallas import tpu as pltpu
from jax.sharding import PartitionSpec as P

HEADS = 8
DH = 64
PAIRS = HEADS // 2
KW = 32
KD = 3
V = 100
VP = 128
FIRST, SECOND = 112, 120
EDGE = 64
OWN = 128
D = 1024
E = HEADS * DH
G = 512
MEMBERS = 8
SHARDS = 64

score_scale = 6.0
eps_norm = 1e-06
delta_smooth = 0.1

MESH = pl.DeviceIdType.MESH
f32 = jnp.float32
bf16 = jnp.bfloat16


def dot(a, b):
    return jnp.dot(a, b, preferred_element_type=f32)


def dot_t(a, b):
    return lax.dot_general(a, b, (((1,), (1,)), ((), ())), preferred_element_type=f32)


def smooth_slope(difference):
    return difference * lax.rsqrt(difference * difference + delta_smooth * delta_smooth)


def head_ones():
    row = lax.broadcasted_iota(jnp.int32, (128, 128), 0) < DH
    lane = lax.broadcasted_iota(jnp.int32, (128, 128), 1) < DH
    return jnp.where(row == lane, 1.0, 0.0).astype(bf16)


def head_means(values, ones):
    low = values.astype(bf16)
    parts = [dot(low[:, 128 * p : 128 * (p + 1)], ones) for p in range(PAIRS)]
    return jnp.concatenate(parts, axis=1) * (1.0 / DH)


def normalize(projected, ones):
    factor = lax.rsqrt(head_means(projected * projected, ones) + eps_norm)
    return projected * factor, factor


def norm_backward(grad_hat, unit_rows, factor, ones):
    return factor * (grad_hat - unit_rows * head_means(grad_hat * unit_rows, ones))


def kernel(
    latent, w_query, w_key, w_value, w_out, w_decode, window, source, edge_weight, target, area,
    out,
    x, xh, wq, wk, wv, wo, wd_raw, wd, win, src, ew, tgt, area_row,
    q_hat, q_factor, k_hat, k_factor, q_low, key_pair, value_pair,
    weight, weight_t, counts2, counts_t, count_send, count_recv, numden, early, early_halo, mixed, mixed_halo, inverse, inverse_halo, numerator_halo,
    pred_rows, spread, gather, truth, fold, base, sums, sums_low, from_left, from_right,
    local_sem, halo_send, halo_recv, member_send, member_recv,
):
    m = lax.axis_index("member")
    s = lax.axis_index("space")
    has_left = s > 0
    has_right = s < SHARDS - 1
    even = lax.rem(s, 2) == 0
    left = (m, lax.rem(s + SHARDS - 1, SHARDS))
    right = (m, lax.rem(s + 1, SHARDS))
    core = lax.rem(m, 2)
    peers = [
        (lax.rem(m - core + d // 2 * 2, MEMBERS) + (core if d % 2 == 0 else 1 - core), s)
        for d in range(MEMBERS)
    ]

    barrier = pltpu.get_barrier_semaphore()

    @pl.when(has_left)
    def _():
        pl.semaphore_signal(barrier, inc=1, device_id=left, device_id_type=MESH)

    @pl.when(has_right)
    def _():
        pl.semaphore_signal(barrier, inc=1, device_id=right, device_id_type=MESH)

    for d in range(1, MEMBERS):
        pl.semaphore_signal(barrier, inc=1, device_id=peers[d], device_id_type=MESH)

    pairs = [
        (latent.at[0], x), (window, win), (w_decode, wd_raw), (w_key, wk), (w_value, wv),
        (w_query, wq), (w_out, wo), (source, src), (edge_weight, ew), (target, tgt),
        (area, area_row),
    ]
    loads = [pltpu.make_async_copy(a, b, local_sem.at[i]) for i, (a, b) in enumerate(pairs)]
    for load in loads:
        load.start()
    (x_load, win_load, wd_load, wk_load, wv_load, wq_load, wo_load, src_load, ew_load, tgt_load,
     area_load) = loads

    @pl.when(jnp.logical_not(has_left))
    def _():
        xh[EDGE:] = jnp.zeros((EDGE, D), bf16)
        count_recv[:EDGE] = jnp.zeros((EDGE, OWN), bf16)
        pred_rows[OWN + EDGE :, :VP] = jnp.zeros((EDGE, VP), bf16)
        early_halo[EDGE:] = jnp.zeros((EDGE, E), bf16)
        from_left[...] = jnp.zeros((2 * EDGE, VP), bf16)

    @pl.when(jnp.logical_not(has_right))
    def _():
        xh[:EDGE] = jnp.zeros((EDGE, D), bf16)
        count_recv[EDGE:] = jnp.zeros((EDGE, OWN), bf16)
        pred_rows[OWN : OWN + EDGE, :VP] = jnp.zeros((EDGE, VP), bf16)
        early_halo[:EDGE] = jnp.zeros((EDGE, E), bf16)
        from_right[...] = jnp.zeros((2 * EDGE, VP), bf16)

    def halo(index, to_left, to_right):
        copies = [
            pltpu.make_async_remote_copy(
                src_ref=a, dst_ref=b, send_sem=halo_send.at[index, side],
                recv_sem=halo_recv.at[index, side], device_id=device, device_id_type=MESH,
            )
            for side, (a, b), device in ((0, to_left, left), (1, to_right, right))
        ]

        def start(in_turn=False):
            @pl.when(jnp.logical_and(has_left, even))
            def _():
                copies[0].start()
                if in_turn:
                    copies[0].wait_send()

            @pl.when(has_right)
            def _():
                copies[1].start()

            if in_turn:

                @pl.when(jnp.logical_not(even))
                def _():
                    @pl.when(has_right)
                    def _():
                        copies[1].wait_send()

            @pl.when(jnp.logical_and(has_left, jnp.logical_not(even)))
            def _():
                copies[0].start()

        def arrive():
            @pl.when(has_right)
            def _():
                copies[0].wait_recv()

            @pl.when(has_left)
            def _():
                copies[1].wait_recv()

        def leave():
            @pl.when(has_left)
            def _():
                copies[0].wait_send()

            @pl.when(has_right)
            def _():
                copies[1].wait_send()

        def leave_rest():
            @pl.when(jnp.logical_and(has_left, jnp.logical_not(even)))
            def _():
                copies[0].wait_send()

            @pl.when(jnp.logical_and(has_right, even))
            def _():
                copies[1].wait_send()

        return start, arrive, leave, leave_rest

    def relay_copies(index, rows):
        return [
            pltpu.make_async_remote_copy(
                src_ref=pred_rows.at[rows, pl.ds(VP * d, VP)],
                dst_ref=pred_rows.at[rows, pl.ds(VP * (d + 1), VP)],
                send_sem=member_send.at[index, d + 1],
                recv_sem=member_recv.at[index, d + 1],
                device_id=peers[1],
                device_id_type=MESH,
            )
            for d in (2, 4, 6)
        ]

    def member_copies(index, rows, slots=range(1, MEMBERS)):
        return [
            pltpu.make_async_remote_copy(
                src_ref=pred_rows.at[rows, pl.ds(0, VP)],
                dst_ref=pred_rows.at[rows, pl.ds(VP * d, VP)],
                send_sem=member_send.at[index, d],
                recv_sem=member_recv.at[index, d],
                device_id=peers[d],
                device_id_type=MESH,
            )
            for d in slots
        ]

    lower, upper = pl.ds(0, EDGE), pl.ds(EDGE, EDGE)
    latent_halo = halo(0, (x.at[lower], xh.at[lower]), (x.at[upper], xh.at[upper]))
    count_halo = halo(
        1, (count_send.at[upper], count_recv.at[upper]), (count_send.at[lower], count_recv.at[lower])
    )
    pred_halo = halo(
        2,
        (pred_rows.at[lower, pl.ds(0, VP)], pred_rows.at[pl.ds(OWN, EDGE), pl.ds(0, VP)]),
        (pred_rows.at[upper, pl.ds(0, VP)], pred_rows.at[pl.ds(OWN + EDGE, EDGE), pl.ds(0, VP)]),
    )
    early_exchange = halo(
        3, (early.at[lower], early_halo.at[lower]), (early.at[upper], early_halo.at[upper])
    )
    sum_exchange = halo(
        4,
        (sums_low.at[pl.ds(OWN + EDGE, 2 * EDGE)], from_right),
        (sums_low.at[pl.ds(EDGE, 2 * EDGE)], from_left),
    )

    x_load.wait()
    one = jnp.int32(1)
    pl.semaphore_wait(
        barrier, MEMBERS - 1 + jnp.minimum(s, one) + jnp.minimum(SHARDS - 1 - s, one)
    )

    latent_halo[0](True)

    ones = head_ones()
    lane = lax.broadcasted_iota(jnp.int32, (128, 128), 1)
    first_head = lane < DH
    first_ones = jnp.where(first_head, 1.0, 0.0).astype(bf16)
    second_ones = jnp.where(first_head, 0.0, 1.0).astype(bf16)

    win_load.wait()
    near = jnp.bitwise_and(win[...] - s * OWN, 255)
    place = lax.broadcasted_iota(jnp.int32, (256, 128), 0)
    turned = jnp.zeros((256, OWN), f32)
    for k in range(KW):
        turned = turned + jnp.where(near[k : k + 1] == place, 1.0, 0.0)
    counts = turned.T
    count_send[...] = turned[OWN:].astype(bf16)
    count_halo[0]()
    own_counts, halo_counts = counts[:, :OWN], counts[:, OWN:]
    counts2[...] = jnp.concatenate([own_counts, own_counts, halo_counts, halo_counts], axis=1)
    counts_t[...] = turned[:OWN]

    def split_pair(values):
        return jnp.concatenate(
            [jnp.where(first_head, values, 0.0), jnp.where(first_head, 0.0, values)], axis=0
        ).astype(bf16)

    def put_keys(rows, where, keep):
        k_unit, k_scale = normalize(dot(rows, wk[...]), ones)
        values = dot(rows, wv[...])
        if keep:
            k_hat[...] = k_unit
            k_factor[...] = k_scale
        for p in range(PAIRS):
            cols = slice(128 * p, 128 * (p + 1))
            key_pair[p, where : where + 256] = split_pair(k_unit[:, cols])
            value_pair[p, where : where + 256, :128] = split_pair(values[:, cols])
            value_pair[p, where : where + 128, 128:] = first_ones
            value_pair[p, where + 128 : where + 256, 128:] = second_ones

    def put_queries(rows, where, keep):
        q_unit, q_scale = normalize(dot(rows, wq[...]), ones)
        if keep:
            q_hat[...] = q_unit
            q_factor[...] = q_scale
        q_low[where : where + OWN] = (q_unit * (score_scale / DH)).astype(bf16)

    own_rows = x[...]
    wk_load.wait()
    wv_load.wait()
    put_keys(own_rows, 0, True)
    wq_load.wait()
    put_queries(own_rows, 0, True)

    def attend(p, where):
        cols = slice(128 * p, 128 * (p + 1))
        scores = dot_t(q_low[:OWN, cols], key_pair[p, where : where + 256])
        chosen = (counts2[:, where : where + 256] * jnp.exp(scores)).astype(bf16)
        weight[p, :, where : where + 256] = chosen
        return dot(chosen, value_pair[p, where : where + 256])

    def attend_turned(p, where, count_turned):
        cols = slice(128 * p, 128 * (p + 1))
        scores = dot_t(key_pair[p, :256], q_low[where : where + OWN, cols])
        twice = jnp.concatenate([count_turned, count_turned], axis=0)
        weight_t[p, :, where : where + OWN] = (twice * jnp.exp(scores)).astype(bf16)

    for p in range(PAIRS):
        both = attend(p, 0)
        numden[p] = both
        early[:, 128 * p : 128 * (p + 1)] = both[:, :128].astype(bf16)

    wd_load.wait()
    wd[...] = jnp.zeros((VP, D), bf16)
    wd[:V] = wd_raw[...]
    base[...] = dot_t(own_rows, wd[...])
    wo_load.wait()
    fold[...] = dot_t(wd[...], wo[...]).astype(bf16)

    src_load.wait()
    ew_load.wait()
    area_load.wait()
    tgt_load.wait()
    for g in range(0, G, 128):
        near = jnp.bitwise_and(src[:, g : g + 128] - s * OWN, 255)
        edges = jnp.zeros((256, 128), f32)
        for k in range(KD):
            edges = edges + jnp.where(near[k : k + 1] == place, ew[k : k + 1, g : g + 128], 0.0)
        gather[g : g + 128] = edges.T.astype(bf16)
        spread[:, g : g + 128] = (edges * area_row[:, g : g + 128]).astype(bf16)
        block = tgt[:, g : g + 128].astype(f32)
        truth[g : g + 128] = jnp.concatenate([block, jnp.zeros((VP - V, 128), f32)], axis=0).T

    for p in range(PAIRS):
        attend_turned(p, 0, counts_t[...])

    latent_halo[3]()

    latent_halo[1]()
    halo_rows = xh[...]
    put_keys(halo_rows, 256, False)
    decoded = base[...]
    for p in range(PAIRS):
        cols = slice(128 * p, 128 * (p + 1))
        both = numden[p] + attend(p, 256)
        recip = 1.0 / both[:, 128:]
        inverse[:, cols] = recip
        mixed[:, cols] = (both[:, :128] * recip).astype(bf16)
        decoded = jnp.where(lane == SECOND + p, recip, decoded)
        decoded = jnp.where(lane == FIRST + p, pltpu.roll(recip, DH, 1), decoded)
    pred_rows[:OWN, :VP] = (decoded + dot_t(mixed[...], fold[...])).astype(bf16)
    pred_halo[0]()
    own_out = member_copies(0, pl.ds(0, OWN), (4, 2, 6, 1))
    for copy in own_out:
        copy.start()
    early_exchange[0]()

    put_queries(halo_rows, OWN, False)
    count_halo[1]()
    crossed = count_recv[...].astype(f32)
    for p in range(PAIRS):
        attend_turned(p, OWN, crossed)
    crossed = crossed.T
    crossed = jnp.concatenate([crossed, crossed], axis=1)
    for p in range(PAIRS):
        scores = dot_t(q_low[OWN:, 128 * p : 128 * (p + 1)], key_pair[p, :256])
        numerator_halo[p] = dot((crossed * jnp.exp(scores)).astype(bf16), value_pair[p, :256, :128])

    pred_halo[1]()
    halo_out = member_copies(1, pl.ds(OWN, OWN), (4, 5, 6, 7, 2, 3, 1))
    for copy in halo_out:
        copy.start()
    for copy in own_out:
        copy.wait_recv()
    own_relay = relay_copies(0, pl.ds(0, OWN))
    for copy in own_relay:
        copy.start()
    early_exchange[1]()
    row = lax.broadcasted_iota(jnp.int32, (128, 128), 0)
    for p in range(PAIRS):
        cols = slice(128 * p, 128 * (p + 1))
        pick = jnp.where(row == jnp.where(first_head, FIRST + p, SECOND + p), 1.0, 0.0).astype(bf16)
        recip = dot(pred_rows[OWN:, :VP], pick)
        inverse_halo[:, cols] = recip
        mixed_halo[:, cols] = (
            (numerator_halo[p] + early_halo[:, cols].astype(f32)) * recip
        ).astype(bf16)
    for copy in own_relay:
        copy.wait_recv()
    for copy in halo_out:
        copy.wait_recv()

    total = jnp.zeros((256, VP), f32)
    for g in range(0, G, 128):
        rows = gather[g : g + 128]
        mine = dot(rows, pred_rows[:, :VP])
        slopes = jnp.zeros((128, VP), f32)
        for d in range(1, MEMBERS):
            slopes = slopes + smooth_slope(mine - dot(rows, pred_rows[:, VP * d : VP * (d + 1)]))
        dpred = smooth_slope(mine - truth[g : g + 128]) - slopes * (1.0 / (MEMBERS - 1))
        total = total + dot(spread[:, g : g + 128], dpred.astype(bf16))
    sums[...] = total
    sums_low[:256] = total.astype(bf16)
    sums_low[256:] = total[:EDGE].astype(bf16)
    sum_exchange[0]()

    sum_exchange[1]()
    near_left = from_left[...].astype(f32)
    near_right = from_right[...].astype(f32)
    own_sum = (
        sums[:OWN] + jnp.concatenate([near_left[EDGE:], near_right[:EDGE]], axis=0)
    ).astype(bf16)
    halo_sum = (
        sums[OWN:] + jnp.concatenate([near_right[EDGE:], near_left[:EDGE]], axis=0)
    ).astype(bf16)

    dmixed = dot(own_sum, fold[...]) * inverse[...]
    dmixed_halo = dot(halo_sum, fold[...]) * inverse_halo[...]
    dmixed_all = jnp.concatenate([dmixed, dmixed_halo], axis=0)
    mixed_all = jnp.concatenate([mixed[...], mixed_halo[...]], axis=0).astype(f32)
    dmixed_low = dmixed_all.astype(bf16)
    row_low = (-dmixed_all * mixed_all).astype(bf16)
    dq_parts, dk_parts, dv_parts = [], [], []
    for p in range(PAIRS):
        cols = slice(128 * p, 128 * (p + 1))
        sides = jnp.concatenate([dmixed_low[:, cols], row_low[:, cols]], axis=1)
        dscore = (weight[p].astype(f32) * dot_t(sides[:OWN], value_pair[p])).astype(bf16)
        dq_parts.append(dot(dscore, key_pair[p]) * (score_scale / DH))
        dscore_t = (weight_t[p].astype(f32) * dot_t(value_pair[p, :256], sides)).astype(bf16)
        dk = dot(dscore_t, q_low[:, cols])
        dv = dot(weight_t[p], dmixed_low[:, cols])
        dk_parts.append(jnp.where(first_head, dk[:OWN], dk[OWN:]))
        dv_parts.append(jnp.where(first_head, dv[:OWN], dv[OWN:]))
    dq = norm_backward(jnp.concatenate(dq_parts, axis=1), q_hat[...], q_factor[...], ones)
    dk = norm_backward(jnp.concatenate(dk_parts, axis=1), k_hat[...], k_factor[...], ones)
    dv = jnp.concatenate(dv_parts, axis=1)
    grad = dot(own_sum, wd[...]) + dot_t(dq.astype(bf16), wq[...])
    grad = grad + dot_t(dk.astype(bf16), wk[...])
    grad = grad + dot_t(dv.astype(bf16), wv[...])
    out[0] = grad.astype(bf16)

    for exchange in (count_halo, pred_halo, early_exchange, sum_exchange):
        exchange[2]()
    for copy in own_out + own_relay + halo_out:
        copy.wait_send()


def per_device(
    latent, w_query, w_key, w_value, w_out, w_decode, window, decoder_src, edge_weight, target, area
):
    vmem = pltpu.VMEM
    hbm = pl.BlockSpec(memory_space=pltpu.HBM)
    return pl.pallas_call(
        kernel,
        out_shape=jax.ShapeDtypeStruct((1, OWN, D), bf16),
        in_specs=[hbm] * 11,
        out_specs=pl.BlockSpec(memory_space=pltpu.VMEM),
        scratch_shapes=[
            vmem((OWN, D), bf16),
            vmem((2 * EDGE, D), bf16),
            vmem((D, E), bf16),
            vmem((D, E), bf16),
            vmem((D, E), bf16),
            vmem((E, D), bf16),
            vmem((V, D), bf16),
            vmem((VP, D), bf16),
            vmem((KW, OWN), jnp.int32),
            vmem((KD, G), jnp.int32),
            vmem((KD, G), f32),
            vmem((V, G), bf16),
            vmem((1, G), f32),
            vmem((OWN, E), f32),
            vmem((OWN, E), f32),
            vmem((OWN, E), f32),
            vmem((OWN, E), f32),
            vmem((2 * OWN, E), bf16),
            vmem((PAIRS, 512, 128), bf16),
            vmem((PAIRS, 512, 256), bf16),
            vmem((PAIRS, OWN, 512), bf16),
            vmem((PAIRS, 256, 256), bf16),
            vmem((OWN, 512), f32),
            vmem((OWN, OWN), f32),
            vmem((OWN, OWN), bf16),
            vmem((OWN, OWN), bf16),
            vmem((PAIRS, OWN, 256), f32),
            vmem((OWN, E), bf16),
            vmem((2 * EDGE, E), bf16),
            vmem((OWN, E), bf16),
            vmem((2 * EDGE, E), bf16),
            vmem((OWN, E), f32),
            vmem((2 * EDGE, E), f32),
            vmem((PAIRS, 2 * EDGE, 128), f32),
            vmem((256, MEMBERS * VP), bf16),
            vmem((256, G), bf16),
            vmem((G, 256), bf16),
            vmem((G, VP), f32),
            vmem((VP, E), bf16),
            vmem((OWN, VP), f32),
            vmem((256, VP), f32),
            vmem((320, VP), bf16),
            vmem((2 * EDGE, VP), bf16),
            vmem((2 * EDGE, VP), bf16),
            pltpu.SemaphoreType.DMA((11,)),
            pltpu.SemaphoreType.DMA((5, 2)),
            pltpu.SemaphoreType.DMA((5, 2)),
            pltpu.SemaphoreType.DMA((2, MEMBERS)),
            pltpu.SemaphoreType.DMA((2, MEMBERS)),
        ],
        compiler_params=pltpu.CompilerParams(
            collective_id=0, has_side_effects=True, vmem_limit_bytes=60 << 20
        ),
    )(
        latent, w_query, w_key, w_value, w_out, w_decode, window.T, decoder_src.T, edge_weight.T,
        target, area.reshape(1, -1),
    )


def solution(mesh):
    in_specs = (
        P("member", "space", None),
        P(),
        P(),
        P(),
        P(),
        P(),
        P("space", None),
        P("space", None),
        P("space", None),
        P(None, "space"),
        P("space"),
    )
    out_specs = P("member", "space", None)
    return jax.shard_map(
        per_device, mesh=mesh, in_specs=in_specs, out_specs=out_specs, check_vma=False
    )
```
